32 devices in a mesh: cases: 2 (over x), bus: 16 (over z, y, core).
Axes of the slice: x: 2, y: 2, z: 4, core: 2. Of those that a mesh axis runs over, the one named last changes fastest.
Arguments:
- ptdf: bfloat16 [20480, 10240], P('bus'), may hold values from -0.078125 to 0.078125
- line_limit: float32 [20480], P('bus'), may hold values from 1 to 8
- gen_cost: float32 [12288], P('bus'), may hold values from 0.1 to 2
- gen_max: float32 [12288], P('bus'), may hold values from 0.5 to 4
- gen_owner: int32 [12288, 1], P('bus'), may hold values from 0 to 15; in each aligned block of 768 rows (0 to 767, 768 to 1535, ...) at most 144 rows name the same one
- gen_local: int32 [12288], P('bus'), may hold values from 0 to 639
- availability: float32 [24576, 128], P(('cases', 'bus')), parts along dimension 0, may hold values from 0 to 1
- demand: float32 [20480, 128], P(('cases', 'bus')), parts along dimension 0, may hold values from 0.5 to 2.5
- dispatch: float32 [24576, 128], P(('cases', 'bus')), parts along dimension 0, may hold values from 0 to 2
- balance_price: float32 [256], P('cases'), parts along dimension 0, may hold values from -6 to 6
- line_price: float32 [40960, 128], P(('cases', 'bus')), parts along dimension 0, may hold values from -4 to 4
Outputs:
- dispatch_out: float32 [24576, 128], P(('cases', 'bus')), parts along dimension 0
- balance_out: float32 [256], P('cases'), parts along dimension 0
- line_out: float32 [40960, 128], P(('cases', 'bus')), parts along dimension 0
The draws below stay inside these ranges and needn't reach their ends.
There are 2 independent parts, one for each index of `cases`. The reference program is written for one: setup_inputs(seed, part) draws one part's arguments, and reference() takes and returns one part's arrays. A program takes and returns all parts, laid end to end along the dimension named above; an argument that names none is the same for every part. Nothing has to cross between parts.
Inputs may be any that keep to these rules, and one draw needn't show every extreme that they name: `gen_owner`: among the 768 generators of one device (aligned blocks of rows), no owner is named more than 144 times, a bound that some block reaches.
All inputs are finite; a program needn't handle non-finite values.
Results may differ from the reference program's by a relative error of at most 0.0036.
Values may be sent and summed in bfloat16 or wider, within the bound.
A program may use at most 128 MiB of HBM per device.

```python
import math
import jax
import jax.numpy as jnp
import numpy as np
from jax import lax

BUSES = 10240
LINES = 20480
HOURS = 128
GEN_DEV = 768
ITERS = 2
GENS = 12288
BUS_DEV = 640
CAP = 144
N_BUS = 16


def place_ends(result, stream_key, least, largest):
    spot = [jax.random.randint(jax.random.fold_in(stream_key, axis), (), 0, length) for axis, length in enumerate(result.shape)]
    longest = result.shape.index(max(result.shape))
    neighbour = spot[:longest] + [(spot[longest] + 1) % result.shape[longest]] + spot[longest + 1:]
    return result.at[tuple(spot)].set(least).at[tuple(neighbour)].set(largest)


def raised(values, own_key, source, target, parts, factor):
    def block_of(dim):
        return (jnp.arange(values.shape[dim]) // (values.shape[dim] // parts)).reshape((-1,) + (1,) * (values.ndim - 1 - dim))

    near = jax.random.permutation(own_key, parts)[block_of(target)]
    other_side = (block_of(target) + parts // 2) % parts
    return jnp.where((block_of(source) == near) | (block_of(source) == other_side), factor * values, values)


def levels(stream_key, extent, pieces, least, largest):
    def one(axis_at, shards_of):
        heights = jax.random.uniform(jax.random.fold_in(jax.random.fold_in(stream_key, 6), axis_at), (shards_of,), jnp.float32, least / len(pieces), largest / len(pieces))
        return jnp.repeat(jnp.exp(heights), extent[axis_at] // shards_of).reshape((-1,) + (1,) * (len(extent) - axis_at - 1))

    level = one(*pieces[0])
    for cut in pieces[1:]:
        level = level * one(*cut)
    return level


def assign_block(key, own, number, rows, amount, top, most, lean):
    sequence = jax.random.permutation(key, amount)
    packed, usual = shares(amount, rows * top, most, lean, True), shares(amount, rows * top, most, lean, False)
    places = jnp.arange(amount)

    def named(tallies, rotation):
        used = int((tallies > 0).sum())
        fixed = max(1, used // 4)
        passed = fixed + (places - fixed + rotation * (used - fixed)) % max(1, amount - fixed)
        return jnp.zeros((amount,), jnp.int32).at[sequence[jnp.where(places < fixed, places, passed)]].set(jnp.asarray(tallies, jnp.int32))

    tallies = jnp.where(number % 4 == 0, named(packed, number // 4), named(usual, number - number // 4 - 1))
    mixed = jax.random.permutation(jax.random.fold_in(own, 3), amount)
    donor, taker = mixed[0:amount // 2 * 2:2], mixed[1:amount // 2 * 2:2]
    room = jnp.minimum(tallies[donor] - 1, most - tallies[taker]) // 2
    room = jnp.where((donor == sequence[0]) | (taker == sequence[0]) | (tallies[taker] == 0), 0, jnp.maximum(room, 0))
    passed = jax.random.randint(jax.random.fold_in(own, 4), (amount // 2,), 0, 1 << 20) % (room + 1)
    tallies = tallies.at[donor].add(-passed).at[taker].add(passed)
    items = jnp.searchsorted(jnp.cumsum(tallies), jnp.arange(rows * top), side="right").astype(jnp.int32)
    listing = items.reshape(top, rows).T
    listing = listing[jax.random.permutation(jax.random.fold_in(own, 1), rows)]
    rotation = jax.random.randint(jax.random.fold_in(own, 2), (rows, 1), 0, top)
    return jnp.take_along_axis(listing, (jnp.arange(top)[None, :] + rotation) % top, axis=1)


def shares(count, total, bound, skew, full):
    weights = [(1 << 20) // math.isqrt(standing ** skew) + 1 for standing in range(1, count + 1)]
    largest = bound if full else min(bound, max(-(-total // count), total * weights[0] // sum(weights)))
    least = 1 if total - largest >= count - 1 else 0
    counts, rest = [largest] + [least] * (count - 1), total - largest - least * (count - 1)
    while rest > 0:
        candidates = [i for i in range(1, count) if counts[i] < largest] or [i for i in range(1, count) if counts[i] < bound]
        whole, left = sum([weights[i] for i in candidates]), rest
        for i in candidates:
            addition = min(bound - counts[i], max(1, left * weights[i] // whole), rest)
            counts[i] = counts[i] + addition
            rest = rest - addition
    return np.array(counts)


def normal_values(rng, dims, scale, most, pieces=(), kind=jnp.bfloat16):
    result = scale * jax.random.normal(rng, dims, jnp.float32)
    if pieces:
        result = result * levels(rng, dims, pieces, -0.22, 0.18)
    return jnp.clip(result, -most, most).astype(kind)


def heavy_noise(rng, extent, scale, most, cuts, heavy, held_as=jnp.bfloat16):
    entries = scale * jax.random.normal(rng, extent, jnp.float32)
    if cuts:
        entries = entries * levels(rng, extent, cuts, -0.22, 0.18)
    return jnp.clip(raised(entries, jax.random.fold_in(rng, 3), *heavy), -most, most).astype(held_as)


def setup_inputs(seed: int = 0, part: int = 0) -> dict:
    key_list = jax.random.split(jax.random.key(seed), 12)
    own_keys = jax.random.split(jax.random.fold_in(key_list[11], part), 12)
    ptdf = heavy_noise(key_list[0], (LINES, BUSES), BUSES ** -0.5, 0.078125, ((0, 16),), (0, 1, 16, 2.0))
    line_limit = jnp.clip(jnp.exp(math.log(8.0) - 2.0794415 * jax.random.uniform(key_list[1], (LINES,), jnp.float32) ** levels(key_list[1], (LINES,), ((0, 16),), -0.2, 0.2)), 1.0, 8.0)
    gen_cost = jnp.clip(jnp.exp(math.log(2.0) - 2.9957323 * jax.random.uniform(key_list[2], (GENS,), jnp.float32) ** levels(key_list[2], (GENS,), ((0, 16),), -0.2, 0.2)), 0.1, 2.0)
    gen_max = jnp.clip(jnp.exp(math.log(4.0) - 2.0794415 * jax.random.uniform(key_list[3], (GENS,), jnp.float32) ** levels(key_list[3], (GENS,), ((0, 16),), -0.2, 0.2)), 0.5, 4.0)
    gen_owner_keys = jax.random.split(jax.random.fold_in(key_list[4], 1), GENS // GEN_DEV)
    gen_owner_turns = jax.random.permutation(jax.random.fold_in(key_list[4], 3), GENS // GEN_DEV)
    gen_owner = jax.vmap(lambda own, number: assign_block(jax.random.fold_in(key_list[4], 2), own, number, GEN_DEV, N_BUS, 1, CAP, 2))(gen_owner_keys, gen_owner_turns).reshape((GENS, 1))
    gen_local = place_ends(jax.random.randint(key_list[5], (GENS,), 0, BUS_DEV), jax.random.fold_in(key_list[5], 1), 0, BUS_DEV - 1).astype(jnp.int32)
    availability = jnp.clip(1.0 * jax.random.uniform(own_keys[6], (GENS, HOURS), jnp.float32) ** levels(own_keys[6], (GENS, HOURS), ((0, 16),), -0.2, 0.2), 0.0, 1.0)
    demand = jnp.clip(0.5 + 2.0 * jax.random.uniform(own_keys[7], (BUSES, HOURS), jnp.float32) ** levels(own_keys[7], (BUSES, HOURS), ((0, 16),), -0.2, 0.2), 0.5, 2.5)
    dispatch = jnp.clip(2.0 * jax.random.uniform(own_keys[8], (GENS, HOURS), jnp.float32) ** levels(own_keys[8], (GENS, HOURS), ((0, 16),), -0.2, 0.2), 0.0, 2.0)
    balance_price = normal_values(own_keys[9], (HOURS,), 1.0, 6.0, (), jnp.float32)
    line_price = normal_values(own_keys[10], (LINES, HOURS), 0.5, 4.0, ((0, 16),), jnp.float32)
    return dict(ptdf=ptdf, line_limit=line_limit, gen_cost=gen_cost, gen_max=gen_max, gen_owner=gen_owner, gen_local=gen_local, availability=availability, demand=demand, dispatch=dispatch, balance_price=balance_price, line_price=line_price)


tau_step = 0.2
sigma_step = 0.15


def reference(ptdf, line_limit, gen_cost, gen_max, gen_owner, gen_local, availability, demand, dispatch, balance_price, line_price):
    bus_count = BUSES // N_BUS
    gen_bus = (gen_owner[:, 0] * bus_count + gen_local).astype(jnp.int32)
    upper = gen_max[:, None] * availability
    limit = line_limit[:, None]
    for iteration in range(ITERS):
        line_half = line_price.astype(jnp.bfloat16)
        shadow = lax.dot_general(ptdf, line_half, (((0,), (0,)), ((), ())), preferred_element_type=jnp.float32)
        price = shadow[gen_bus] + balance_price[None, :]
        updated = jnp.clip(dispatch - tau_step * (gen_cost[:, None] + price), 0.0, upper)
        extra = 2.0 * updated - dispatch
        injection = jax.ops.segment_sum(extra, gen_bus, num_segments=BUSES) - demand
        balance = jnp.sum(injection, axis=0)
        balance_price = balance_price + sigma_step * balance / BUSES
        flow = jnp.dot(ptdf, injection.astype(jnp.bfloat16), preferred_element_type=jnp.float32)
        shifted = line_price + sigma_step * flow
        line_price = shifted - sigma_step * jnp.clip(shifted / sigma_step, -limit, limit)
        dispatch = updated
    return (dispatch, balance_price, line_price)
```

```python
import functools

import jax
import jax.numpy as jnp
from jax import lax
from jax.experimental import pallas as pl
from jax.experimental.pallas import tpu as pltpu
from jax.sharding import PartitionSpec as P

ITERS = 2


tau_step = 0.2
sigma_step = 0.15

BF = jnp.bfloat16
F32 = jnp.float32
NT = (((1,), (1,)), ((), ()))
TN = (((0,), (0,)), ((), ()))


def dot(a, b, dims=(((1,), (0,)), ((), ()))):
    return lax.dot_general(a, b, dims, preferred_element_type=F32)


def split(x):
    high = x.astype(BF)
    return high, (x - high.astype(F32)).astype(BF)


def loop(low, high, body):
    lax.fori_loop(low, high, lambda i, c: (body(i), c)[1], 0)


def kernel(
    n,
    capacity,
    flat,
    ptdf,
    limit,
    gen_rows_in,
    gen_max,
    availability,
    demand,
    dispatch,
    balance_in,
    line_in,
    dispatch_out,
    balance_out,
    line_out,
    pt,
    line_t,
    part_tx,
    part,
    core_rx,
    y_tx,
    y_rx,
    z_tx,
    z_rx,
    shadow_t,
    inj_all,
    inj_acc,
    flow,
    bal,
    pick,
    gen_tx,
    gen_rx,
    seat,
    cost,
    upper,
    state,
    ret_tx,
    ret_rx,
    load_sem,
    s1,
    r1,
    s2,
    r2,
    s3,
    r3,
    s4,
    r4,
    s5,
    r5,
    s6,
    r6,
    sa,
    ra,
    sb,
    rb,
):
    lines = pt.shape[1]
    buses = pt.shape[2]
    hours = line_in.shape[1]
    gens = dispatch.shape[0]
    wide = gen_tx.shape[2]
    depth = n // 4
    me = lax.axis_index("bus")
    c = lax.rem(me, 2)
    y = lax.rem(lax.div(me, 2), 2)
    z = lax.div(me, 4)

    def at(zz, yy, cc):
        return zz * 4 + yy * 2 + cc

    def z_to(k):
        return lax.rem(z + 1 + k, depth)

    def z_from(k):
        return lax.rem(z + 2 * depth - 1 - k, depth)

    core_peer = at(z, y, 1 - c)
    y_peer = at(z, 1 - y, c)

    def load(o):
        if flat:
            src = ptdf.at[:, pl.ds(pl.multiple_of(o * buses, 128), buses)]
        else:
            src = ptdf.at[o]
        return pltpu.make_async_copy(src, pt.at[o], load_sem.at[o])

    def remote(src, dst, send, recv, target):
        return pltpu.make_async_remote_copy(
            src_ref=src,
            dst_ref=dst,
            send_sem=send,
            recv_sem=recv,
            device_id={"bus": target},
            device_id_type=pl.DeviceIdType.MESH,
        )

    def owners(k):
        zt = z_to(k)
        return (at(zt, 1 - y, 1 - c), at(zt, 1 - y, c), at(zt, y, 1 - c), at(zt, y, c))

    def start_loads(k):
        a, b, _, _ = owners(k)
        load(a).start()
        load(b).start()

    def start_loads_near(k):
        _, _, a, b = owners(k)
        load(a).start()
        load(b).start()

    loop(0, depth, start_loads)
    loop(0, depth, start_loads_near)

    barrier = pltpu.get_barrier_semaphore()

    def greet(d):
        pl.semaphore_signal(
            barrier,
            inc=1,
            device_id={"bus": lax.rem(me + d, n)},
            device_id_type=pl.DeviceIdType.MESH,
        )

    loop(1, n, greet)
    pl.semaphore_wait(barrier, n - 1)

    line_out[...] = line_in[...]
    balance_out[...] = balance_in[...]

    owner_row = gen_rows_in[0:1, :]
    local_row = gen_rows_in[1:2, :]
    cost_row = gen_rows_in[2:3, :]
    owner_ids = lax.broadcasted_iota(jnp.int32, (n, gens), 0).astype(F32)
    hits = (owner_ids == owner_row).astype(F32)
    before = (
        lax.broadcasted_iota(jnp.int32, (gens, gens), 0)
        < lax.broadcasted_iota(jnp.int32, (gens, gens), 1)
    ).astype(F32)
    counts = dot(hits.astype(BF), before.astype(BF))
    rank_row = jnp.sum(counts * hits, axis=0, keepdims=True)
    local_high = jnp.floor(local_row * (1.0 / 16.0))
    local_low = local_row - 16.0 * local_high
    cost_a = cost_row.astype(BF).astype(F32)
    cost_b = (cost_row - cost_a).astype(BF).astype(F32)
    cost_c = cost_row - cost_a - cost_b
    facts = jnp.concatenate(
        [
            local_high,
            local_low,
            jnp.ones_like(local_row),
            cost_a,
            cost_b,
            cost_c,
            jnp.zeros((10, gens), F32),
        ],
        axis=0,
    ).astype(BF)
    goods = jnp.concatenate(
        [dispatch[...].astype(BF), (gen_max[...] * availability[...]).astype(BF)], axis=1
    )
    slot_ids = lax.broadcasted_iota(jnp.int32, (wide, gens), 0).astype(F32)

    def gen_copy(d):
        return remote(
            gen_tx.at[d], gen_rx.at[d], sa.at[d], ra.at[d], lax.rem(me + d, n)
        )

    def send_gens(d):
        o = lax.rem(me + d, n).astype(F32)
        where = jnp.where(owner_row == o, rank_row, -1.0)
        chosen = (slot_ids == where).astype(F32).astype(BF)
        pick[d] = chosen[:capacity]
        body = dot(chosen[:capacity], goods).astype(BF)
        tail = dot(facts, chosen, NT).astype(BF)

        @pl.when(d > 0)
        def _():
            gen_tx[d, :capacity] = body
            gen_tx[d, capacity:] = tail
            gen_copy(d).start()

        @pl.when(d == 0)
        def _():
            gen_rx[0, :capacity] = body
            gen_rx[0, capacity:] = tail

    loop(0, n, send_gens)

    def take_gens(d):
        @pl.when(d > 0)
        def _():
            gen_copy(d).wait_recv()

        eye = (
            lax.broadcasted_iota(jnp.int32, (capacity, wide), 0)
            == lax.broadcasted_iota(jnp.int32, (capacity, wide), 1)
        ).astype(F32).astype(BF)
        columns = dot(eye, gen_rx[d, capacity:], NT)
        bus = jnp.where(
            columns[:, 2:3] > 0.5, columns[:, 0:1] * 16.0 + columns[:, 1:2], -1.0
        )
        ids = lax.broadcasted_iota(jnp.int32, (capacity, buses), 1).astype(F32)
        seat[d] = (ids == bus).astype(F32).astype(BF)
        cost[d] = jnp.broadcast_to(
            columns[:, 3:4] + columns[:, 4:5] + columns[:, 5:6], (capacity, hours)
        )
        state[d] = gen_rx[d, :capacity, :hours].astype(F32)
        upper[d] = gen_rx[d, :capacity, hours:].astype(F32)

    def c1(j):
        return remote(part_tx.at[j], core_rx.at[j], s1.at[j], r1.at[j], core_peer)

    def c2(k):
        return remote(y_tx.at[k], y_rx.at[k], s2.at[k], r2.at[k], y_peer)

    def c3(k):
        return remote(z_tx.at[k], z_rx.at[k], s3.at[k], r3.at[k], at(z_to(k), y, c))

    def c4(k):
        own = inj_all.at[me]
        return remote(own, own, s4.at[k], r4.at[k], at(z_to(k), y, c))

    def c5(k):
        block = inj_all.at[at(z_from(k), y, c)]
        return remote(block, block, s5.at[k], r5.at[k], y_peer)

    def c6(k):
        block = inj_all.at[at(z_from(k), y, c)]
        return remote(block, block, s6.at[k], r6.at[k], core_peer)

    def c6y(k):
        block = inj_all.at[at(z_from(k), 1 - y, c)]
        return remote(block, block, s6.at[depth + k], r6.at[depth + k], core_peer)

    def ret_copy(d):
        return remote(
            ret_tx.at[d], ret_rx.at[d], sb.at[d], rb.at[d], lax.rem(me + n - d, n)
        )

    def iterate(it):
        line_t[...] = jnp.transpose(line_out[...]).astype(BF)

        def partial(o):
            @pl.when(it == 0)
            def _():
                load(o).wait()

            return dot(line_t[...], pt[o])

        def step(j, send_to, keep):
            part_tx[j] = partial(send_to).astype(BF)
            c1(j).start()
            part[j] = partial(keep)

        def far_finish(k):
            c1(k).wait_recv()
            y_tx[k] = (part[k] + core_rx[k].astype(F32)).astype(BF)
            c2(k).start()

        def far(k):
            a, b, _, _ = owners(k)
            step(k, a, b)

            @pl.when(k > 0)
            def _():
                far_finish(k - 1)

        def near(k):
            _, _, a, b = owners(k)
            step(depth + k, a, b)

            @pl.when(k == 0)
            def _():
                far_finish(depth - 1)

        def near_finish(k):
            c1(depth + k).wait_recv()
            c2(k).wait_recv()
            total = (
                part[depth + k]
                + core_rx[depth + k].astype(F32)
                + y_rx[k].astype(F32)
            )

            @pl.when(k < depth - 1)
            def _():
                z_tx[k] = total.astype(BF)
                c3(k).start()

            @pl.when(k == depth - 1)
            def _():
                shadow_t[...] = total

        loop(0, depth, far)
        loop(0, depth, near)
        loop(0, depth, near_finish)

        @pl.when(it == 0)
        def _():
            loop(0, n, take_gens)

        def add_z(k):
            c3(k).wait_recv()
            shadow_t[...] += z_rx[k].astype(F32)

        loop(0, depth - 1, add_z)

        def sent_rs(k):
            c1(k).wait_send()
            c1(depth + k).wait_send()
            c2(k).wait_send()

        loop(0, depth, sent_rs)
        loop(0, depth - 1, lambda k: c3(k).wait_send())

        high, low = split(shadow_t[...])
        both = jnp.concatenate([high, low], axis=0)
        inj_acc[...] = jnp.zeros_like(inj_acc)

        def update(d):
            found = dot(seat[d], both, NT)
            price = found[:, :hours] + found[:, hours:] + balance_out[...]
            now = state[d]
            updated = jnp.clip(now - tau_step * (cost[d] + price), 0.0, upper[d])
            high, low = split(2.0 * updated - now)
            inj_acc[...] += dot(seat[d], jnp.concatenate([high, low], axis=1), TN)
            state[d] = updated

            @pl.when(it == ITERS - 1)
            def _():
                @pl.when(d > 0)
                def _():
                    ret_tx[d] = updated.astype(BF)

                @pl.when(d == 0)
                def _():
                    ret_rx[0] = updated.astype(BF)

        loop(0, n, update)
        inj_all[me] = (inj_acc[:, :hours] + inj_acc[:, hours:] - demand[...]).astype(BF)

        loop(0, depth - 1, lambda k: c4(k).start())
        c5(depth - 1).start()
        c6(depth - 1).start()

        @pl.when(it == ITERS - 1)
        def _():
            loop(1, n, lambda d: ret_copy(d).start())

        flow[...] = jnp.zeros_like(flow)
        bal[...] = jnp.zeros_like(bal)
        tile = lines // 5

        def use(o):
            block = inj_all[o]
            bal[...] += jnp.sum(
                block.astype(F32).reshape(buses // 8, 8, hours), axis=0
            )

            def rows(i):
                here = pl.ds(pl.multiple_of(i * tile, tile), tile)
                flow[here, :] += dot(pt[o, here, :], block)

            loop(0, 5, rows)

        def y_part(k):
            c5(k).wait_recv()
            c6y(k).start()
            use(at(z_from(k), 1 - y, c))
            c6y(k).wait_recv()
            use(at(z_from(k), 1 - y, 1 - c))

        use(me)
        c6(depth - 1).wait_recv()
        use(at(z, y, 1 - c))

        def arrive(k):
            @pl.when(k < depth - 1)
            def _():
                c4(k).wait_recv()
                c5(k).start()
                c6(k).start()
                use(at(z_from(k), y, c))

            y_part(lax.rem(k + depth - 1, depth))

            @pl.when(k < depth - 1)
            def _():
                c6(k).wait_recv()
                use(at(z_from(k), y, 1 - c))

        loop(0, depth, arrive)

        shifted = line_out[...] + sigma_step * flow[...]
        bound = limit[...]
        line_out[...] = shifted - sigma_step * jnp.clip(
            shifted / sigma_step, -bound, bound
        )
        balance_out[...] = balance_out[...] + sigma_step * jnp.sum(
            bal[...], axis=0, keepdims=True
        ) / (n * buses)

        loop(0, depth - 1, lambda k: c4(k).wait_send())

        def sent_ag(k):
            c5(k).wait_send()
            c6(k).wait_send()
            c6y(k).wait_send()

        loop(0, depth, sent_ag)

    loop(0, ITERS, iterate)

    dispatch_out[...] = jnp.zeros_like(dispatch_out)

    def collect(d):
        @pl.when(d > 0)
        def _():
            ret_copy(d).wait_recv()

        dispatch_out[...] += dot(pick[d], ret_rx[d], TN)

    loop(0, n, collect)

    def sent(d):
        gen_copy(d).wait_send()
        ret_copy(d).wait_send()

    loop(1, n, sent)


def local(
    ptdf,
    line_limit,
    gen_cost,
    gen_max,
    gen_owner,
    gen_local,
    availability,
    demand,
    dispatch,
    balance_price,
    line_price,
):
    n = lax.axis_size("bus")
    buses = demand.shape[0]
    lines, hours = line_price.shape
    gens = dispatch.shape[0]
    capacity = -(-max(2, 3 * gens // n) // 16) * 16
    wide = max(2 * hours, -(-capacity // 128) * 128)
    depth = n // 4
    flat = buses % 128 == 0
    if not flat:
        ptdf = ptdf.reshape(lines, n, buses).transpose(1, 0, 2)
    gen_rows = jnp.concatenate(
        [
            gen_owner.reshape(1, gens).astype(F32),
            gen_local.reshape(1, gens).astype(F32),
            gen_cost.reshape(1, gens),
            jnp.zeros((5, gens), F32),
        ],
        axis=0,
    )
    vmem = pl.BlockSpec(memory_space=pltpu.VMEM)
    dma = pltpu.SemaphoreType.DMA
    block = (hours, buses)
    out = pl.pallas_call(
        functools.partial(kernel, n, capacity, flat),
        out_shape=(
            jax.ShapeDtypeStruct((gens, hours), F32),
            jax.ShapeDtypeStruct((1, hours), F32),
            jax.ShapeDtypeStruct((lines, hours), F32),
        ),
        in_specs=[pl.BlockSpec(memory_space=pl.ANY)] + [vmem] * 8,
        out_specs=(vmem, vmem, vmem),
        scratch_shapes=[
            pltpu.VMEM((n, lines, buses), BF),
            pltpu.VMEM((hours, lines), BF),
            pltpu.VMEM((2 * depth,) + block, BF),
            pltpu.VMEM((2 * depth,) + block, F32),
            pltpu.VMEM((2 * depth,) + block, BF),
            pltpu.VMEM((depth,) + block, BF),
            pltpu.VMEM((depth,) + block, BF),
            pltpu.VMEM((depth,) + block, BF),
            pltpu.VMEM((depth,) + block, BF),
            pltpu.VMEM(block, F32),
            pltpu.VMEM((n, buses, hours), BF),
            pltpu.VMEM((buses, 2 * hours), F32),
            pltpu.VMEM((lines, hours), F32),
            pltpu.VMEM((8, hours), F32),
            pltpu.VMEM((n, capacity, gens), BF),
            pltpu.VMEM((n, capacity + 16, wide), BF),
            pltpu.VMEM((n, capacity + 16, wide), BF),
            pltpu.VMEM((n, capacity, buses), BF),
            pltpu.VMEM((n, capacity, hours), F32),
            pltpu.VMEM((n, capacity, hours), F32),
            pltpu.VMEM((n, capacity, hours), F32),
            pltpu.VMEM((n, capacity, hours), BF),
            pltpu.VMEM((n, capacity, hours), BF),
            dma((n,)),
            dma((2 * depth,)),
            dma((2 * depth,)),
        ]
        + [dma((depth,))] * 8
        + [dma((2 * depth,))] * 2
        + [dma((n,))] * 4,
        compiler_params=pltpu.CompilerParams(
            collective_id=0, has_side_effects=True, vmem_limit_bytes=63 * 1024 * 1024
        ),
    )(
        ptdf,
        line_limit[:, None],
        gen_rows,
        gen_max[:, None],
        availability,
        demand,
        dispatch,
        balance_price[None, :],
        line_price,
    )
    return out[0], out[1][0], out[2]


def solution(mesh):
    return jax.shard_map(
        local,
        mesh=mesh,
        in_specs=(
            P("bus", None),
            P("bus"),
            P("bus"),
            P("bus"),
            P("bus", None),
            P("bus"),
            P(("cases", "bus"), None),
            P(("cases", "bus"), None),
            P(("cases", "bus"), None),
            P("cases"),
            P(("cases", "bus"), None),
        ),
        out_specs=(P(("cases", "bus"), None), P("cases"), P(("cases", "bus"), None)),
        check_vma=False,
    )
```

```python
import functools

import jax
import jax.numpy as jnp
from jax import lax
from jax.experimental import pallas as pl
from jax.experimental.pallas import tpu as pltpu
from jax.sharding import PartitionSpec as P

ITERS = 2


tau_step = 0.2
sigma_step = 0.15

BF = jnp.bfloat16
F32 = jnp.float32
NT = (((1,), (1,)), ((), ()))
TN = (((0,), (0,)), ((), ()))


def dot(a, b, dims=(((1,), (0,)), ((), ()))):
    return lax.dot_general(a, b, dims, preferred_element_type=F32)


def split(x):
    high = x.astype(BF)
    return high, (x - high.astype(F32)).astype(BF)


def loop(low, high, body):
    lax.fori_loop(low, high, lambda i, c: (body(i), c)[1], 0)


def kernel(
    n,
    capacity,
    flat,
    ptdf,
    limit,
    gen_rows_in,
    availability,
    demand,
    dispatch,
    balance_in,
    line_in,
    dispatch_out,
    balance_out,
    line_out,
    pt,
    line_t,
    part_tx,
    part,
    core_rx,
    y_tx,
    y_rx,
    z_tx,
    z_rx,
    shadow_t,
    inj_all,
    ext,
    line_now,
    flow,
    bal,
    pick,
    gen_tx,
    gen_rx,
    seat,
    cost,
    upper,
    state,
    ret_tx,
    ret_rx,
    load_sem,
    s1,
    r1,
    s2,
    r2,
    s3,
    r3,
    s4,
    r4,
    s5,
    r5,
    s6,
    r6,
    sa,
    ra,
    sb,
    rb,
):
    lines = pt.shape[1]
    buses = pt.shape[2]
    hours = line_in.shape[1]
    chunk = n // 4 * (gen_tx.shape[1] - 16)
    gens = dispatch.shape[0]
    wide = gen_tx.shape[2]
    depth = n // 4
    me = lax.axis_index("bus")
    c = lax.rem(me, 2)
    y = lax.rem(lax.div(me, 2), 2)
    z = lax.div(me, 4)

    def at(zz, yy, cc):
        return zz * 4 + yy * 2 + cc

    def z_to(k):
        return lax.rem(z + 1 + k, depth)

    def z_from(k):
        return lax.rem(z + 2 * depth - 1 - k, depth)

    core_peer = at(z, y, 1 - c)
    y_peer = at(z, 1 - y, c)

    def load(o):
        if flat:
            src = ptdf.at[:, pl.ds(pl.multiple_of(o * buses, 128), buses)]
        else:
            src = ptdf.at[o]
        return pltpu.make_async_copy(src, pt.at[o], load_sem.at[o])

    def remote(src, dst, send, recv, target):
        return pltpu.make_async_remote_copy(
            src_ref=src,
            dst_ref=dst,
            send_sem=send,
            recv_sem=recv,
            device_id={"bus": target},
            device_id_type=pl.DeviceIdType.MESH,
        )

    def owners(k):
        zt = z_to(k)
        return (at(zt, 1 - y, 1 - c), at(zt, 1 - y, c), at(zt, y, 1 - c), at(zt, y, c))

    def start_loads(k):
        a, b, _, _ = owners(k)
        load(a).start()
        load(b).start()

    def start_loads_near(k):
        _, _, a, b = owners(k)
        load(a).start()
        load(b).start()

    loop(0, depth, start_loads)
    loop(0, depth, start_loads_near)

    barrier = pltpu.get_barrier_semaphore()

    def greet(d):
        pl.semaphore_signal(
            barrier,
            inc=1,
            device_id={"bus": lax.rem(me + d, n)},
            device_id_type=pl.DeviceIdType.MESH,
        )

    loop(1, n, greet)
    pl.semaphore_wait(barrier, n - 1)

    line_now[...] = jnp.transpose(line_in[...])
    balance_out[...] = balance_in[...]

    owner_row = gen_rows_in[0:1, :]
    local_row = gen_rows_in[1:2, :]
    cost_row = gen_rows_in[2:3, :]
    top_row = gen_rows_in[3:4, :]
    owner_ids = lax.broadcasted_iota(jnp.int32, (n, gens), 0).astype(F32)
    hits = (owner_ids == owner_row).astype(F32)
    before = (
        lax.broadcasted_iota(jnp.int32, (gens, gens), 0)
        < lax.broadcasted_iota(jnp.int32, (gens, gens), 1)
    ).astype(F32)
    counts = dot(hits.astype(BF), before.astype(BF))
    rank_row = jnp.sum(counts * hits, axis=0, keepdims=True)
    local_high = jnp.floor(local_row * (1.0 / 16.0))
    local_low = local_row - 16.0 * local_high

    def parts(x):
        a = x.astype(BF).astype(F32)
        b = (x - a).astype(BF).astype(F32)
        return [a, b, x - a - b]

    facts = jnp.concatenate(
        [
            local_high,
            local_low,
            jnp.ones_like(local_row),
            *parts(cost_row),
            *parts(top_row),
            jnp.zeros((7, gens), F32),
        ],
        axis=0,
    ).astype(BF)
    goods = jnp.concatenate(
        [dispatch[...].astype(BF), availability[...].astype(BF)], axis=1
    )
    slot_ids = lax.broadcasted_iota(jnp.int32, (wide, gens), 0).astype(F32)

    def rows_of(d):
        return pl.ds(pl.multiple_of(d * capacity, 16), capacity)

    def chunk_of(q):
        return pl.ds(pl.multiple_of(q * chunk, 16), chunk)

    def gen_copy(d):
        return remote(
            gen_tx.at[d], gen_rx.at[d], sa.at[d], ra.at[d], lax.rem(me + d, n)
        )

    def send_gens(q):
        def choose(i):
            d = q * depth + i
            o = lax.rem(me + d, n).astype(F32)
            where = jnp.where(owner_row == o, rank_row, -1.0)
            chosen = (slot_ids == where).astype(F32).astype(BF)
            pick[rows_of(d), :] = chosen[:capacity]
            gen_tx[d, capacity:] = dot(facts, chosen, NT).astype(BF)

        loop(0, depth, choose)
        body = dot(pick[chunk_of(q), :], goods).astype(BF)
        for i in range(depth):
            gen_tx[q * depth + i, :capacity] = body[i * capacity : (i + 1) * capacity]

        def start(i):
            d = q * depth + i

            @pl.when(d > 0)
            def _():
                gen_copy(d).start()

            @pl.when(d == 0)
            def _():
                gen_rx[0] = gen_tx[0]

        loop(0, depth, start)

    loop(0, 4, send_gens)

    def take_gens(d):
        @pl.when(d > 0)
        def _():
            gen_copy(d).wait_recv()

        eye = (
            lax.broadcasted_iota(jnp.int32, (capacity, wide), 0)
            == lax.broadcasted_iota(jnp.int32, (capacity, wide), 1)
        ).astype(F32).astype(BF)
        columns = dot(eye, gen_rx[d, capacity:], NT)
        bus = jnp.where(
            columns[:, 2:3] > 0.5, columns[:, 0:1] * 16.0 + columns[:, 1:2], -1.0
        )
        ids = lax.broadcasted_iota(jnp.int32, (capacity, buses), 1).astype(F32)
        here = rows_of(d)
        seat[here, :] = (ids == bus).astype(F32).astype(BF)
        cost[here, :] = jnp.broadcast_to(
            columns[:, 3:4] + columns[:, 4:5] + columns[:, 5:6], (capacity, hours)
        )
        top = columns[:, 6:7] + columns[:, 7:8] + columns[:, 8:9]
        state[here, :] = gen_rx[d, :capacity, :hours].astype(F32)
        upper[here, :] = top * gen_rx[d, :capacity, hours:].astype(F32)

    def c1(j):
        return remote(part_tx.at[j], core_rx.at[j], s1.at[j], r1.at[j], core_peer)

    def c2(k):
        return remote(y_tx.at[k], y_rx.at[k], s2.at[k], r2.at[k], y_peer)

    def c3(k):
        return remote(z_tx.at[k], z_rx.at[k], s3.at[k], r3.at[k], at(z_to(k), y, c))

    def c4(k):
        own = inj_all.at[me]
        return remote(own, own, s4.at[k], r4.at[k], at(z_to(k), y, c))

    def c5(k):
        block = inj_all.at[at(z_from(k), y, c)]
        return remote(block, block, s5.at[k], r5.at[k], y_peer)

    def c6(k):
        block = inj_all.at[at(z_from(k), y, c)]
        return remote(block, block, s6.at[k], r6.at[k], core_peer)

    def c6y(k):
        block = inj_all.at[at(z_from(k), 1 - y, c)]
        return remote(block, block, s6.at[depth + k], r6.at[depth + k], core_peer)

    def ret_copy(d):
        return remote(
            ret_tx.at[rows_of(d), :],
            ret_rx.at[rows_of(d), :],
            sb.at[d],
            rb.at[d],
            lax.rem(me + n - d, n),
        )

    def iterate(it):
        line_t[...] = line_now[...].astype(BF)

        def partial(o):
            @pl.when(it == 0)
            def _():
                load(o).wait()

            return dot(line_t[...], pt[o])

        def step(j, send_to, keep):
            part_tx[j] = partial(send_to).astype(BF)
            c1(j).start()
            part[j] = partial(keep)

        def far_finish(k):
            c1(k).wait_recv()
            y_tx[k] = (part[k] + core_rx[k].astype(F32)).astype(BF)
            c2(k).start()

        def far(k):
            a, b, _, _ = owners(k)
            step(k, a, b)

            @pl.when(k > 0)
            def _():
                far_finish(k - 1)

        def near(k):
            _, _, a, b = owners(k)
            step(depth + k, a, b)

            @pl.when(k == 0)
            def _():
                far_finish(depth - 1)

        def near_finish(k):
            c1(depth + k).wait_recv()
            c2(k).wait_recv()
            total = (
                part[depth + k]
                + core_rx[depth + k].astype(F32)
                + y_rx[k].astype(F32)
            )

            @pl.when(k < depth - 1)
            def _():
                z_tx[k] = total.astype(BF)
                c3(k).start()

            @pl.when(k == depth - 1)
            def _():
                shadow_t[...] = total

        loop(0, depth, far)
        loop(0, depth, near)
        loop(0, depth, near_finish)

        @pl.when(it == 0)
        def _():
            loop(0, n, take_gens)

        def add_z(k):
            c3(k).wait_recv()
            shadow_t[...] += z_rx[k].astype(F32)

        loop(0, depth - 1, add_z)

        def sent_rs(k):
            c1(k).wait_send()
            c1(depth + k).wait_send()
            c2(k).wait_send()

        loop(0, depth, sent_rs)
        loop(0, depth - 1, lambda k: c3(k).wait_send())

        high, low = split(shadow_t[...])
        both = jnp.concatenate([high, low], axis=0)

        def update(q):
            here = chunk_of(q)
            found = dot(seat[here, :], both, NT)
            price = found[:, :hours] + found[:, hours:] + balance_out[...]
            now = state[here, :]
            updated = jnp.clip(
                now - tau_step * (cost[here, :] + price), 0.0, upper[here, :]
            )
            high, low = split(2.0 * updated - now)
            ext[here, :] = jnp.concatenate([high, low], axis=1)
            state[here, :] = updated

            @pl.when(it == ITERS - 1)
            def _():
                ret_tx[here, :] = updated.astype(BF)

        loop(0, 4, update)
        made = dot(ext[...], seat[...], TN)
        inj_all[me] = (made[:hours] + made[hours:] - jnp.transpose(demand[...])).astype(
            BF
        )

        loop(0, depth - 1, lambda k: c4(k).start())
        c5(depth - 1).start()
        c6(depth - 1).start()

        @pl.when(it == ITERS - 1)
        def _():
            ret_rx[:capacity, :] = ret_tx[:capacity, :]
            loop(1, n, lambda d: ret_copy(d).start())

        flow[...] = jnp.zeros_like(flow)
        bal[...] = jnp.zeros_like(bal)

        def use(o):
            block = inj_all[o]
            bal[...] += block.astype(F32)
            flow[...] += dot(block, pt[o], NT)

        def y_part(k):
            c5(k).wait_recv()
            c6y(k).start()
            use(at(z_from(k), 1 - y, c))
            c6y(k).wait_recv()
            use(at(z_from(k), 1 - y, 1 - c))

        use(me)
        c6(depth - 1).wait_recv()
        use(at(z, y, 1 - c))

        def arrive(k):
            @pl.when(k < depth - 1)
            def _():
                c4(k).wait_recv()
                c5(k).start()
                c6(k).start()
                use(at(z_from(k), y, c))

            y_part(lax.rem(k + depth - 1, depth))

            @pl.when(k < depth - 1)
            def _():
                c6(k).wait_recv()
                use(at(z_from(k), y, 1 - c))

        loop(0, depth, arrive)

        shifted = line_now[...] + sigma_step * flow[...]
        bound = limit[...]
        line_now[...] = shifted - sigma_step * jnp.clip(
            shifted / sigma_step, -bound, bound
        )
        surplus = jnp.sum(jnp.transpose(bal[...]), axis=0, keepdims=True)
        balance_out[...] = balance_out[...] + sigma_step * surplus / (n * buses)

        loop(0, depth - 1, lambda k: c4(k).wait_send())

        def sent_ag(k):
            c5(k).wait_send()
            c6(k).wait_send()
            c6y(k).wait_send()

        loop(0, depth, sent_ag)

    loop(0, ITERS, iterate)

    line_out[...] = jnp.transpose(line_now[...])
    loop(1, n, lambda d: ret_copy(d).wait_recv())
    dispatch_out[...] = jnp.transpose(dot(ret_rx[...], pick[...], TN))

    def sent(d):
        gen_copy(d).wait_send()
        ret_copy(d).wait_send()

    loop(1, n, sent)


def local(
    ptdf,
    line_limit,
    gen_cost,
    gen_max,
    gen_owner,
    gen_local,
    availability,
    demand,
    dispatch,
    balance_price,
    line_price,
):
    n = lax.axis_size("bus")
    buses = demand.shape[0]
    lines, hours = line_price.shape
    gens = dispatch.shape[0]
    capacity = -(-max(2, 3 * gens // n) // 16) * 16
    wide = max(2 * hours, -(-capacity // 128) * 128)
    depth = n // 4
    flat = buses % 128 == 0
    if not flat:
        ptdf = ptdf.reshape(lines, n, buses).transpose(1, 0, 2)
    gen_rows = jnp.concatenate(
        [
            gen_owner.reshape(1, gens).astype(F32),
            gen_local.reshape(1, gens).astype(F32),
            gen_cost.reshape(1, gens),
            gen_max.reshape(1, gens),
            jnp.zeros((4, gens), F32),
        ],
        axis=0,
    )
    vmem = pl.BlockSpec(memory_space=pltpu.VMEM)
    dma = pltpu.SemaphoreType.DMA
    block = (hours, buses)
    out = pl.pallas_call(
        functools.partial(kernel, n, capacity, flat),
        out_shape=(
            jax.ShapeDtypeStruct((gens, hours), F32),
            jax.ShapeDtypeStruct((1, hours), F32),
            jax.ShapeDtypeStruct((lines, hours), F32),
        ),
        in_specs=[pl.BlockSpec(memory_space=pl.ANY)] + [vmem] * 7,
        out_specs=(vmem, vmem, vmem),
        scratch_shapes=[
            pltpu.VMEM((n, lines, buses), BF),
            pltpu.VMEM((hours, lines), BF),
            pltpu.VMEM((2 * depth,) + block, BF),
            pltpu.VMEM((2 * depth,) + block, F32),
            pltpu.VMEM((2 * depth,) + block, BF),
            pltpu.VMEM((depth,) + block, BF),
            pltpu.VMEM((depth,) + block, BF),
            pltpu.VMEM((depth,) + block, BF),
            pltpu.VMEM((depth,) + block, BF),
            pltpu.VMEM(block, F32),
            pltpu.VMEM((n,) + block, BF),
            pltpu.VMEM((n * capacity, 2 * hours), BF),
            pltpu.VMEM((hours, lines), F32),
            pltpu.VMEM((hours, lines), F32),
            pltpu.VMEM(block, F32),
            pltpu.VMEM((n * capacity, gens), BF),
            pltpu.VMEM((n, capacity + 16, wide), BF),
            pltpu.VMEM((n, capacity + 16, wide), BF),
            pltpu.VMEM((n * capacity, buses), BF),
            pltpu.VMEM((n * capacity, hours), F32),
            pltpu.VMEM((n * capacity, hours), F32),
            pltpu.VMEM((n * capacity, hours), F32),
            pltpu.VMEM((n * capacity, hours), BF),
            pltpu.VMEM((n * capacity, hours), BF),
            dma((n,)),
            dma((2 * depth,)),
            dma((2 * depth,)),
        ]
        + [dma((depth,))] * 8
        + [dma((2 * depth,))] * 2
        + [dma((n,))] * 4,
        compiler_params=pltpu.CompilerParams(
            collective_id=0, has_side_effects=True, vmem_limit_bytes=63 * 1024 * 1024
        ),
    )(
        ptdf,
        line_limit[None, :],
        gen_rows,
        availability,
        demand,
        dispatch,
        balance_price[None, :],
        line_price,
    )
    return out[0], out[1][0], out[2]


def solution(mesh):
    return jax.shard_map(
        local,
        mesh=mesh,
        in_specs=(
            P("bus", None),
            P("bus"),
            P("bus"),
            P("bus"),
            P("bus", None),
            P("bus"),
            P(("cases", "bus"), None),
            P(("cases", "bus"), None),
            P(("cases", "bus"), None),
            P("cases"),
            P(("cases", "bus"), None),
        ),
        out_specs=(P(("cases", "bus"), None), P("cases"), P(("cases", "bus"), None)),
        check_vma=False,
    )
```

```python
import functools

import jax
import jax.numpy as jnp
from jax import lax
from jax.experimental import pallas as pl
from jax.experimental.pallas import tpu as pltpu
from jax.sharding import PartitionSpec as P

ITERS = 2


tau_step = 0.2
sigma_step = 0.15

BF = jnp.bfloat16
F32 = jnp.float32
NT = (((1,), (1,)), ((), ()))
TN = (((0,), (0,)), ((), ()))


def dot(a, b, dims=(((1,), (0,)), ((), ()))):
    return lax.dot_general(a, b, dims, preferred_element_type=F32)


def split(x):
    high = x.astype(BF)
    return high, (x - high.astype(F32)).astype(BF)


def loop(low, high, body):
    lax.fori_loop(low, high, lambda i, c: (body(i), c)[1], 0)


def kernel(
    n,
    capacity,
    flat,
    ptdf,
    limit,
    gen_rows_in,
    availability,
    demand,
    dispatch,
    balance_in,
    line_in,
    dispatch_out,
    balance_out,
    line_out,
    pt,
    line_t,
    part_tx,
    part,
    core_rx,
    y_tx,
    y_rx,
    z_tx,
    z_rx,
    shadow_t,
    inj_all,
    ext,
    line_now,
    flow,
    bal,
    pick,
    gen_tx,
    gen_rx,
    seat,
    cost,
    upper,
    state,
    ret_tx,
    ret_rx,
    load_sem,
    s1,
    r1,
    s2,
    r2,
    s3,
    r3,
    s4,
    r4,
    s5,
    r5,
    s6,
    r6,
    sa,
    ra,
    sb,
    rb,
):
    lines = pt.shape[1]
    buses = pt.shape[2]
    hours = line_in.shape[1]
    chunk = n // 4 * (gen_tx.shape[1] - 16)
    gens = dispatch.shape[0]
    wide = gen_tx.shape[2]
    depth = n // 4
    me = lax.axis_index("bus")
    c = lax.rem(me, 2)
    y = lax.rem(lax.div(me, 2), 2)
    z = lax.div(me, 4)

    def at(zz, yy, cc):
        return zz * 4 + yy * 2 + cc

    def z_to(k):
        return lax.rem(z + 1 + k, depth)

    def z_from(k):
        return lax.rem(z + 2 * depth - 1 - k, depth)

    core_peer = at(z, y, 1 - c)
    y_peer = at(z, 1 - y, c)

    def load(o):
        if flat:
            src = ptdf.at[:, pl.ds(pl.multiple_of(o * buses, 128), buses)]
        else:
            src = ptdf.at[o]
        return pltpu.make_async_copy(src, pt.at[o], load_sem.at[o])

    def remote(src, dst, send, recv, target):
        return pltpu.make_async_remote_copy(
            src_ref=src,
            dst_ref=dst,
            send_sem=send,
            recv_sem=recv,
            device_id={"bus": target},
            device_id_type=pl.DeviceIdType.MESH,
        )

    def owners(k):
        zt = z_to(k)
        return (at(zt, 1 - y, 1 - c), at(zt, 1 - y, c), at(zt, y, 1 - c), at(zt, y, c))

    def start_loads(k):
        a, b, _, _ = owners(k)
        load(a).start()
        load(b).start()

    def start_loads_near(k):
        _, _, a, b = owners(k)
        load(a).start()
        load(b).start()

    loop(0, depth, start_loads)
    loop(0, depth, start_loads_near)

    barrier = pltpu.get_barrier_semaphore()

    def greet(d):
        pl.semaphore_signal(
            barrier,
            inc=1,
            device_id={"bus": lax.rem(me + d, n)},
            device_id_type=pl.DeviceIdType.MESH,
        )

    loop(1, n, greet)
    pl.semaphore_wait(barrier, n - 1)

    line_now[...] = jnp.transpose(line_in[...])
    balance_out[...] = balance_in[...]

    owner_row = gen_rows_in[0:1, :]
    local_row = gen_rows_in[1:2, :]
    cost_row = gen_rows_in[2:3, :]
    top_row = gen_rows_in[3:4, :]
    owner_ids = lax.broadcasted_iota(jnp.int32, (n, gens), 0).astype(F32)
    hits = (owner_ids == owner_row).astype(F32)
    before = (
        lax.broadcasted_iota(jnp.int32, (gens, gens), 0)
        < lax.broadcasted_iota(jnp.int32, (gens, gens), 1)
    ).astype(F32)
    counts = dot(hits.astype(BF), before.astype(BF))
    rank_row = jnp.sum(counts * hits, axis=0, keepdims=True)
    local_high = jnp.floor(local_row * (1.0 / 16.0))
    local_low = local_row - 16.0 * local_high

    def parts(x):
        a = x.astype(BF).astype(F32)
        b = (x - a).astype(BF).astype(F32)
        return [a, b, x - a - b]

    facts = jnp.concatenate(
        [
            local_high,
            local_low,
            jnp.ones_like(local_row),
            *parts(cost_row),
            *parts(top_row),
            jnp.zeros((7, gens), F32),
        ],
        axis=0,
    ).astype(BF)
    goods = jnp.concatenate(
        [dispatch[...].astype(BF), availability[...].astype(BF)], axis=1
    )
    slot_ids = lax.broadcasted_iota(jnp.int32, (wide, gens), 0).astype(F32)

    def rows_of(d):
        return pl.ds(pl.multiple_of(d * capacity, 16), capacity)

    def chunk_of(q):
        return pl.ds(pl.multiple_of(q * chunk, 16), chunk)

    def gen_copy(d):
        return remote(
            gen_tx.at[d], gen_rx.at[d], sa.at[d], ra.at[d], lax.rem(me + d, n)
        )

    def send_gens(q):
        def choose(i):
            d = q * depth + i
            o = lax.rem(me + d, n).astype(F32)
            where = jnp.where(owner_row == o, rank_row, -1.0)
            chosen = (slot_ids == where).astype(F32).astype(BF)
            pick[rows_of(d), :] = chosen[:capacity]
            gen_tx[d, capacity:] = dot(facts, chosen, NT).astype(BF)

        loop(0, depth, choose)
        body = dot(pick[chunk_of(q), :], goods).astype(BF)
        for i in range(depth):
            gen_tx[q * depth + i, :capacity] = body[i * capacity : (i + 1) * capacity]

        def start(i):
            d = q * depth + i

            @pl.when(d > 0)
            def _():
                gen_copy(d).start()

            @pl.when(d == 0)
            def _():
                gen_rx[0] = gen_tx[0]

        loop(0, depth, start)

    def take_gens(d):
        @pl.when(d > 0)
        def _():
            gen_copy(d).wait_recv()

        eye = (
            lax.broadcasted_iota(jnp.int32, (capacity, wide), 0)
            == lax.broadcasted_iota(jnp.int32, (capacity, wide), 1)
        ).astype(F32).astype(BF)
        columns = dot(eye, gen_rx[d, capacity:], NT)
        bus = jnp.where(
            columns[:, 2:3] > 0.5, columns[:, 0:1] * 16.0 + columns[:, 1:2], -1.0
        )
        ids = lax.broadcasted_iota(jnp.int32, (capacity, buses), 1).astype(F32)
        here = rows_of(d)
        seat[here, :] = (ids == bus).astype(F32).astype(BF)
        cost[here, :] = jnp.broadcast_to(
            columns[:, 3:4] + columns[:, 4:5] + columns[:, 5:6], (capacity, hours)
        )
        top = columns[:, 6:7] + columns[:, 7:8] + columns[:, 8:9]
        state[here, :] = gen_rx[d, :capacity, :hours].astype(F32)
        upper[here, :] = top * gen_rx[d, :capacity, hours:].astype(F32)

    def c1(j):
        return remote(part_tx.at[j], core_rx.at[j], s1.at[j], r1.at[j], core_peer)

    def c2(k):
        return remote(y_tx.at[k], y_rx.at[k], s2.at[k], r2.at[k], y_peer)

    def c3(k):
        return remote(z_tx.at[k], z_rx.at[k], s3.at[k], r3.at[k], at(z_to(k), y, c))

    def c4(k):
        own = inj_all.at[me]
        return remote(own, own, s4.at[k], r4.at[k], at(z_to(k), y, c))

    def c5(k):
        block = inj_all.at[at(z_from(k), y, c)]
        return remote(block, block, s5.at[k], r5.at[k], y_peer)

    def c6(k):
        block = inj_all.at[at(z_from(k), y, c)]
        return remote(block, block, s6.at[k], r6.at[k], core_peer)

    def c6y(k):
        block = inj_all.at[at(z_from(k), 1 - y, c)]
        return remote(block, block, s6.at[depth + k], r6.at[depth + k], core_peer)

    def ret_copy(d):
        return remote(
            ret_tx.at[rows_of(d), :],
            ret_rx.at[rows_of(d), :],
            sb.at[d],
            rb.at[d],
            lax.rem(me + n - d, n),
        )

    def iterate(it):
        line_t[...] = line_now[...].astype(BF)

        def partial(o):
            @pl.when(it == 0)
            def _():
                load(o).wait()

            return dot(line_t[...], pt[o])

        def step(j, send_to, keep):
            part_tx[j] = partial(send_to).astype(BF)
            c1(j).start()
            part[j] = partial(keep)

        def far_finish(k):
            c1(k).wait_recv()
            y_tx[k] = (part[k] + core_rx[k].astype(F32)).astype(BF)
            c2(k).start()

        def far(k):
            a, b, _, _ = owners(k)
            step(k, a, b)

            @pl.when(k > 0)
            def _():
                far_finish(k - 1)

        def near(k):
            _, _, a, b = owners(k)
            step(depth + k, a, b)

            @pl.when(k == 0)
            def _():
                far_finish(depth - 1)

        def near_finish(k):
            c1(depth + k).wait_recv()
            c2(k).wait_recv()
            total = (
                part[depth + k]
                + core_rx[depth + k].astype(F32)
                + y_rx[k].astype(F32)
            )

            @pl.when(k < depth - 1)
            def _():
                z_tx[k] = total.astype(BF)
                c3(k).start()

            @pl.when(k == depth - 1)
            def _():
                shadow_t[...] = total

        loop(0, depth, far)

        @pl.when(it == 0)
        def _():
            loop(0, 4, send_gens)

        loop(0, depth, near)
        loop(0, depth, near_finish)

        @pl.when(it == 0)
        def _():
            loop(0, n, take_gens)

        def add_z(k):
            c3(k).wait_recv()
            shadow_t[...] += z_rx[k].astype(F32)

        loop(0, depth - 1, add_z)

        def sent_rs(k):
            c1(k).wait_send()
            c1(depth + k).wait_send()
            c2(k).wait_send()

        loop(0, depth, sent_rs)
        loop(0, depth - 1, lambda k: c3(k).wait_send())

        high, low = split(shadow_t[...])
        both = jnp.concatenate([high, low], axis=0)

        def update(q):
            here = chunk_of(q)
            found = dot(seat[here, :], both, NT)
            price = found[:, :hours] + found[:, hours:] + balance_out[...]
            now = state[here, :]
            updated = jnp.clip(
                now - tau_step * (cost[here, :] + price), 0.0, upper[here, :]
            )
            high, low = split(2.0 * updated - now)
            ext[here, :] = jnp.concatenate([high, low], axis=1)
            state[here, :] = updated

            @pl.when(it == ITERS - 1)
            def _():
                ret_tx[here, :] = updated.astype(BF)

        loop(0, 4, update)
        made = dot(ext[...], seat[...], TN)
        inj_all[me] = (made[:hours] + made[hours:] - jnp.transpose(demand[...])).astype(
            BF
        )

        loop(0, depth - 1, lambda k: c4(k).start())
        c5(depth - 1).start()
        c6(depth - 1).start()

        @pl.when(it == ITERS - 1)
        def _():
            ret_rx[:capacity, :] = ret_tx[:capacity, :]
            loop(1, n, lambda d: ret_copy(d).start())

        flow[...] = jnp.zeros_like(flow)
        bal[...] = jnp.zeros_like(bal)

        def use(o):
            block = inj_all[o]
            bal[...] += block.astype(F32)
            flow[...] += dot(block, pt[o], NT)

        def y_part(k):
            c5(k).wait_recv()
            c6y(k).start()
            use(at(z_from(k), 1 - y, c))
            c6y(k).wait_recv()
            use(at(z_from(k), 1 - y, 1 - c))

        use(me)
        c6(depth - 1).wait_recv()
        use(at(z, y, 1 - c))

        def arrive(k):
            @pl.when(k < depth - 1)
            def _():
                c4(k).wait_recv()
                c5(k).start()
                c6(k).start()
                use(at(z_from(k), y, c))

            y_part(lax.rem(k + depth - 1, depth))

            @pl.when(k < depth - 1)
            def _():
                c6(k).wait_recv()
                use(at(z_from(k), y, 1 - c))

        loop(0, depth, arrive)

        shifted = line_now[...] + sigma_step * flow[...]
        bound = limit[...]
        line_now[...] = shifted - sigma_step * jnp.clip(
            shifted / sigma_step, -bound, bound
        )
        surplus = jnp.sum(jnp.transpose(bal[...]), axis=0, keepdims=True)
        balance_out[...] = balance_out[...] + sigma_step * surplus / (n * buses)

        loop(0, depth - 1, lambda k: c4(k).wait_send())

        def sent_ag(k):
            c5(k).wait_send()
            c6(k).wait_send()
            c6y(k).wait_send()

        loop(0, depth, sent_ag)

    loop(0, ITERS, iterate)

    line_out[...] = jnp.transpose(line_now[...])
    loop(1, n, lambda d: ret_copy(d).wait_recv())
    dispatch_out[...] = jnp.transpose(dot(ret_rx[...], pick[...], TN))

    def sent(d):
        gen_copy(d).wait_send()
        ret_copy(d).wait_send()

    loop(1, n, sent)


def local(
    ptdf,
    line_limit,
    gen_cost,
    gen_max,
    gen_owner,
    gen_local,
    availability,
    demand,
    dispatch,
    balance_price,
    line_price,
):
    n = lax.axis_size("bus")
    buses = demand.shape[0]
    lines, hours = line_price.shape
    gens = dispatch.shape[0]
    capacity = -(-max(2, 3 * gens // n) // 16) * 16
    wide = max(2 * hours, -(-capacity // 128) * 128)
    depth = n // 4
    flat = buses % 128 == 0
    if not flat:
        ptdf = ptdf.reshape(lines, n, buses).transpose(1, 0, 2)
    gen_rows = jnp.concatenate(
        [
            gen_owner.reshape(1, gens).astype(F32),
            gen_local.reshape(1, gens).astype(F32),
            gen_cost.reshape(1, gens),
            gen_max.reshape(1, gens),
            jnp.zeros((4, gens), F32),
        ],
        axis=0,
    )
    vmem = pl.BlockSpec(memory_space=pltpu.VMEM)
    dma = pltpu.SemaphoreType.DMA
    block = (hours, buses)
    out = pl.pallas_call(
        functools.partial(kernel, n, capacity, flat),
        out_shape=(
            jax.ShapeDtypeStruct((gens, hours), F32),
            jax.ShapeDtypeStruct((1, hours), F32),
            jax.ShapeDtypeStruct((lines, hours), F32),
        ),
        in_specs=[pl.BlockSpec(memory_space=pl.ANY)] + [vmem] * 7,
        out_specs=(vmem, vmem, vmem),
        scratch_shapes=[
            pltpu.VMEM((n, lines, buses), BF),
            pltpu.VMEM((hours, lines), BF),
            pltpu.VMEM((2 * depth,) + block, BF),
            pltpu.VMEM((2 * depth,) + block, F32),
            pltpu.VMEM((2 * depth,) + block, BF),
            pltpu.VMEM((depth,) + block, BF),
            pltpu.VMEM((depth,) + block, BF),
            pltpu.VMEM((depth,) + block, BF),
            pltpu.VMEM((depth,) + block, BF),
            pltpu.VMEM(block, F32),
            pltpu.VMEM((n,) + block, BF),
            pltpu.VMEM((n * capacity, 2 * hours), BF),
            pltpu.VMEM((hours, lines), F32),
            pltpu.VMEM((hours, lines), F32),
            pltpu.VMEM(block, F32),
            pltpu.VMEM((n * capacity, gens), BF),
            pltpu.VMEM((n, capacity + 16, wide), BF),
            pltpu.VMEM((n, capacity + 16, wide), BF),
            pltpu.VMEM((n * capacity, buses), BF),
            pltpu.VMEM((n * capacity, hours), F32),
            pltpu.VMEM((n * capacity, hours), F32),
            pltpu.VMEM((n * capacity, hours), F32),
            pltpu.VMEM((n * capacity, hours), BF),
            pltpu.VMEM((n * capacity, hours), BF),
            dma((n,)),
            dma((2 * depth,)),
            dma((2 * depth,)),
        ]
        + [dma((depth,))] * 8
        + [dma((2 * depth,))] * 2
        + [dma((n,))] * 4,
        compiler_params=pltpu.CompilerParams(
            collective_id=0, has_side_effects=True, vmem_limit_bytes=63 * 1024 * 1024
        ),
    )(
        ptdf,
        line_limit[None, :],
        gen_rows,
        availability,
        demand,
        dispatch,
        balance_price[None, :],
        line_price,
    )
    return out[0], out[1][0], out[2]


def solution(mesh):
    return jax.shard_map(
        local,
        mesh=mesh,
        in_specs=(
            P("bus", None),
            P("bus"),
            P("bus"),
            P("bus"),
            P("bus", None),
            P("bus"),
            P(("cases", "bus"), None),
            P(("cases", "bus"), None),
            P(("cases", "bus"), None),
            P("cases"),
            P(("cases", "bus"), None),
        ),
        out_specs=(P(("cases", "bus"), None), P("cases"), P(("cases", "bus"), None)),
        check_vma=False,
    )
```
